32 devices in a mesh: dp: 16 (over z, y, x), mp: 2 (over core).
Axes of the slice: x: 2, y: 2, z: 4, core: 2. Of those that a mesh axis runs over, the one named last changes fastest.
Arguments:
- forget_rows: bfloat16 [512, 8192], P('dp', 'mp'), may hold values from -6 to 6
- cotangent: bfloat16 [512, 8192], P('dp', 'mp'), may hold values from -6 to 6
- retain_rows: bfloat16 [512, 8192], P('dp', 'mp'), may hold values from -6 to 6
- w_gate: bfloat16 [8192, 16384], P('mp', 'dp'), may hold values from -5 to 5
- w_up: bfloat16 [8192, 16384], P('mp', 'dp'), may hold values from -5 to 5
- w_down: bfloat16 [16384, 8192], P('dp', 'mp'), may hold values from -5 to 5
Outputs:
- retained: bfloat16 [512, 8192], P('dp', 'mp')
- new_gate: bfloat16 [8192, 16384], P('mp', 'dp')
- new_up: bfloat16 [8192, 16384], P('mp', 'dp')
- new_down: bfloat16 [16384, 8192], P('dp', 'mp')
The draws below stay inside these ranges and needn't reach their ends.
All inputs are finite; a program needn't handle non-finite values.
Results may differ from the reference program's by a relative error of at most 0.0071.
Values may be sent and summed in bfloat16 or wider, within the bound.
A program may use at most 192 MiB of HBM per device.

```python
import math
import jax
import jax.numpy as jnp

D = 8192
FF = 16384
TOKENS = 512


def levels(rng, shape, split, low, largest):
    def one(dim, blocks):
        steps = jax.random.uniform(jax.random.fold_in(jax.random.fold_in(rng, 6), dim), (blocks,), jnp.float32, low / len(split), largest / len(split))
        return jnp.repeat(jnp.exp(steps), shape[dim] // blocks).reshape((-1,) + (1,) * (len(shape) - dim - 1))

    loudness = one(*split[0])
    for cut in split[1:]:
        loudness = loudness * one(*cut)
    return loudness


def scatter_about(stream_key, shape, scale, most, cuts=(), kind=jnp.bfloat16):
    entries = scale * jax.random.normal(stream_key, shape, jnp.float32)
    if cuts:
        entries = entries * levels(stream_key, shape, cuts, -0.22, 0.18)
    return jnp.clip(entries, -most, most).astype(kind)


def setup_inputs(seed: int = 0) -> dict:
    splits = jax.random.split(jax.random.key(seed), 7)
    forget_rows = scatter_about(splits[0], (TOKENS, D), 1.0, 6.0, ((0, 16), (1, 2)))
    cotangent = scatter_about(splits[1], (TOKENS, D), 1.0, 6.0, ((0, 16), (1, 2)))
    retain_rows = scatter_about(splits[2], (TOKENS, D), 1.0, 6.0, ((0, 16), (1, 2)))
    w_gate = scatter_about(splits[3], (D, FF), 1.0, 5.0, ((0, 2), (1, 16)))
    w_up = scatter_about(splits[4], (D, FF), 1.0, 5.0, ((0, 2), (1, 16)))
    w_down = scatter_about(splits[5], (FF, D), 1.0, 5.0, ((0, 16), (1, 2)))
    return dict(forget_rows=forget_rows, cotangent=cotangent, retain_rows=retain_rows, w_gate=w_gate, w_up=w_up, w_down=w_down)


STEP_SIZE = 0.5

def unit_forward(rows, gate_weight, up_weight):
    width_scale = 1.0 / math.sqrt(D)
    gate_sum = jnp.dot(rows, gate_weight, preferred_element_type=jnp.float32) * width_scale
    up_sum = jnp.dot(rows, up_weight, preferred_element_type=jnp.float32) * width_scale
    sigmoid_gate = jax.nn.sigmoid(gate_sum)
    return (gate_sum, up_sum, sigmoid_gate, gate_sum * sigmoid_gate)

def reference(forget_rows, cotangent, retain_rows, w_gate, w_up, w_down):
    token_scale = 1.0 / math.sqrt(TOKENS)
    gate_sum, up_sum, sigmoid_gate, active = unit_forward(forget_rows, w_gate, w_up)
    hidden = (active * up_sum).astype(jnp.bfloat16)
    grad_down = jnp.dot(hidden.T, cotangent, preferred_element_type=jnp.float32) * token_scale
    new_down = (w_down.astype(jnp.float32) + STEP_SIZE * grad_down).astype(jnp.bfloat16)
    back_units = jnp.dot(cotangent, w_down.T, preferred_element_type=jnp.float32) * (1.0 / math.sqrt(D))
    grad_gate_units = (back_units * up_sum * sigmoid_gate * (1.0 + gate_sum * (1.0 - sigmoid_gate))).astype(jnp.bfloat16)
    grad_up_units = (back_units * active).astype(jnp.bfloat16)
    grad_gate = jnp.dot(forget_rows.T, grad_gate_units, preferred_element_type=jnp.float32) * token_scale
    new_gate = (w_gate.astype(jnp.float32) + STEP_SIZE * grad_gate).astype(jnp.bfloat16)
    grad_up = jnp.dot(forget_rows.T, grad_up_units, preferred_element_type=jnp.float32) * token_scale
    new_up = (w_up.astype(jnp.float32) + STEP_SIZE * grad_up).astype(jnp.bfloat16)
    gate_keep, up_keep, sigmoid_keep, active_keep = unit_forward(retain_rows, new_gate, new_up)
    hidden_keep = (active_keep * up_keep).astype(jnp.bfloat16)
    retained = jnp.dot(hidden_keep, new_down, preferred_element_type=jnp.float32) * (1.0 / math.sqrt(FF))
    return (retained.astype(jnp.bfloat16), new_gate, new_up, new_down)
```

```python
import math

import jax
import jax.numpy as jnp
from jax import lax
from jax.sharding import PartitionSpec as P

D = 8192
FF = 16384


STEP_SIZE = 0.5

CONTRACT_ROWS = (((0,), (0,)), ((), ()))
CONTRACT_COLS = (((1,), (1,)), ((), ()))


def swap(values, axis, bit):
    size = lax.axis_size(axis)
    return lax.ppermute(values, axis, [(i, i ^ bit) for i in range(size)])


def bit_orders(size):
    bits = [1 << k for k in reversed(range(size.bit_length() - 1))]
    return bits, bits[:-2] + bits[:-3:-1]


def gather_rows(rows, order):
    for bit in order:
        rows = jnp.concatenate([rows, swap(rows, "dp", bit)], axis=0)
    return rows


def gather_halves(rows, orders):
    half = rows.shape[0] // 2
    return [gather_rows(rows[:half], orders[0]), gather_rows(rows[half:], orders[1])]


def sum_features(values):
    if lax.axis_size("mp") != 2:
        return lax.psum_scatter(values, "mp", scatter_dimension=0, tiled=True)
    half = values.shape[0] // 2
    first = lax.axis_index("mp") == 0
    low, high = values[:half], values[half:]
    return jnp.where(first, low, high) + swap(jnp.where(first, high, low), "mp", 1)


def gather_units(values):
    if lax.axis_size("mp") != 2:
        return lax.all_gather(values, "mp", axis=0, tiled=True)
    other = swap(values, "mp", 1)
    first = lax.axis_index("mp") == 0
    return jnp.concatenate([jnp.where(first, values, other), jnp.where(first, other, values)], axis=0)


def project(rows, weight):
    return jnp.dot(rows, weight, preferred_element_type=jnp.float32) * (1.0 / math.sqrt(D))


def body(forget_rows, cotangent, retain_rows, w_gate, w_up, w_down):
    orders = bit_orders(lax.axis_size("dp"))
    total_rows = forget_rows.shape[0] * lax.axis_size("dp")
    token_scale = 1.0 / math.sqrt(total_rows)
    forget = gather_halves(forget_rows, orders)
    cotan = gather_halves(cotangent, orders)
    retain = gather_halves(retain_rows, orders)

    hidden_all, dgate_all, dup_all = [], [], []
    for rows, cot in zip(forget, cotan):
        gate_sum = sum_features(project(rows, w_gate))
        up_sum = sum_features(project(rows, w_up))
        sigmoid_gate = jax.nn.sigmoid(gate_sum)
        active = gate_sum * sigmoid_gate
        hidden_all.append(gather_units((active * up_sum).astype(jnp.bfloat16)))
        back = sum_features(
            lax.dot_general(cot, w_down, CONTRACT_COLS, preferred_element_type=jnp.float32)
            * (1.0 / math.sqrt(D))
        )
        dgate = back * up_sum * sigmoid_gate * (1.0 + gate_sum * (1.0 - sigmoid_gate))
        dgate_all.append(gather_units(dgate.astype(jnp.bfloat16)))
        dup_all.append(gather_units((back * active).astype(jnp.bfloat16)))

    def ascend(weight, left, right):
        grad = (
            lax.dot_general(left, right, CONTRACT_ROWS, preferred_element_type=jnp.float32)
            * token_scale
        )
        return (weight.astype(jnp.float32) + STEP_SIZE * grad).astype(jnp.bfloat16)

    forget_all = jnp.concatenate(forget, axis=0)
    cotan_all = jnp.concatenate(cotan, axis=0)
    new_gate = ascend(w_gate, forget_all, jnp.concatenate(dgate_all, axis=0))
    new_up = ascend(w_up, forget_all, jnp.concatenate(dup_all, axis=0))
    new_down = ascend(w_down, jnp.concatenate(hidden_all, axis=0), cotan_all)

    hidden_keep = []
    for rows in retain:
        gate_keep = sum_features(project(rows, new_gate))
        up_keep = sum_features(project(rows, new_up))
        keep = (gate_keep * jax.nn.sigmoid(gate_keep) * up_keep).astype(jnp.bfloat16)
        hidden_keep.append(gather_units(keep))

    out_scale = 1.0 / math.sqrt(FF)
    half = hidden_keep[0].shape[0] // 2
    near = jnp.concatenate([rows[:half] for rows in hidden_keep], axis=0)
    far = jnp.concatenate([rows[half:] for rows in hidden_keep], axis=0)
    columns = new_down.shape[1]
    step = columns // 2
    pieces = []
    for start in range(0, columns, step):
        weight = new_down[:, start : start + step]
        sent = (jnp.dot(far, weight, preferred_element_type=jnp.float32) * out_scale).astype(
            jnp.bfloat16
        )
        moved = [
            swap(sent[k * half : (k + 1) * half], "dp", order[-1])
            for k, order in enumerate(orders)
        ]
        total = jnp.dot(near, weight, preferred_element_type=jnp.float32) * out_scale
        piece = []
        for k, order in enumerate(orders):
            mine = total[k * half : (k + 1) * half] + moved[k].astype(jnp.float32)
            for bit in reversed(order[:-1]):
                middle = mine.shape[0] // 2
                other = swap(mine[middle:].astype(jnp.bfloat16), "dp", bit)
                mine = mine[:middle] + other.astype(jnp.float32)
            piece.append(mine)
        pieces.append(jnp.concatenate(piece, axis=0))
    retained = jnp.concatenate(pieces, axis=1).astype(jnp.bfloat16)
    return (retained, new_gate, new_up, new_down)


def solution(mesh):
    in_specs = (
        P("dp", "mp"),
        P("dp", "mp"),
        P("dp", "mp"),
        P("mp", "dp"),
        P("mp", "dp"),
        P("dp", "mp"),
    )
    out_specs = (P("dp", "mp"), P("mp", "dp"), P("mp", "dp"), P("dp", "mp"))
    return jax.shard_map(body, mesh=mesh, in_specs=in_specs, out_specs=out_specs, check_vma=False)
```

```python
import math

import jax
import jax.numpy as jnp
from jax import lax
from jax.sharding import PartitionSpec as P

D = 8192
FF = 16384


STEP_SIZE = 0.5

CONTRACT_ROWS = (((0,), (0,)), ((), ()))
CONTRACT_COLS = (((1,), (1,)), ((), ()))


def swap(values, axis, bit):
    size = lax.axis_size(axis)
    return lax.ppermute(values, axis, [(i, i ^ bit) for i in range(size)])


def bit_orders(size):
    bits = [1 << k for k in reversed(range(size.bit_length() - 1))]
    return bits, bits[:-2] + bits[:-3:-1]


def exchange_rows(halves, orders, stage):
    return tuple(
        jnp.concatenate([rows, swap(rows, "dp", order[stage])], axis=0)
        for rows, order in zip(halves, orders)
    )


def split_halves(rows):
    half = rows.shape[0] // 2
    return rows[:half], rows[half:]


def sum_features(values):
    if lax.axis_size("mp") != 2:
        return lax.psum_scatter(values, "mp", scatter_dimension=0, tiled=True)
    half = values.shape[0] // 2
    first = lax.axis_index("mp") == 0
    low, high = values[:half], values[half:]
    return jnp.where(first, low, high) + swap(jnp.where(first, high, low), "mp", 1)


def gather_units(values):
    if lax.axis_size("mp") != 2:
        return lax.all_gather(values, "mp", axis=0, tiled=True)
    other = swap(values, "mp", 1)
    first = lax.axis_index("mp") == 0
    return jnp.concatenate([jnp.where(first, values, other), jnp.where(first, other, values)], axis=0)


def project(rows, weight):
    return jnp.dot(rows, weight, preferred_element_type=jnp.float32) * (1.0 / math.sqrt(D))


def body(forget_rows, cotangent, retain_rows, w_gate, w_up, w_down):
    orders = bit_orders(lax.axis_size("dp"))
    total_rows = forget_rows.shape[0] * lax.axis_size("dp")
    token_scale = 1.0 / math.sqrt(total_rows)
    forget, cotan, retain = map(split_halves, (forget_rows, cotangent, retain_rows))
    stages = len(orders[0])
    early = stages - 2
    for stage in range(early):
        forget = exchange_rows(forget, orders, stage)
        forget, cotan, retain = lax.optimization_barrier((forget, cotan, retain))
    for step in range(max(2, early)):
        if step < 2:
            forget = exchange_rows(forget, orders, early + step)
        if step < early:
            cotan = exchange_rows(cotan, orders, step)
        forget, cotan, retain = lax.optimization_barrier((forget, cotan, retain))
    for step in range(max(2, early)):
        if step < 2:
            cotan = exchange_rows(cotan, orders, early + step)
        if step < early:
            retain = exchange_rows(retain, orders, step)
        cotan, retain = lax.optimization_barrier((cotan, retain))
    for stage in range(early, stages):
        retain = exchange_rows(retain, orders, stage)

    units = w_gate.shape[1]

    def gate_and_up(rows, gate, up):
        sums = sum_features(jnp.concatenate([project(rows, gate), project(rows, up)], axis=1))
        return sums[:, :units], sums[:, units:]

    hidden_all, grads_all = [], []
    for rows, cot in zip(forget, cotan):
        gate_sum, up_sum = gate_and_up(rows, w_gate, w_up)
        sigmoid_gate = jax.nn.sigmoid(gate_sum)
        active = gate_sum * sigmoid_gate
        hidden_all.append(gather_units((active * up_sum).astype(jnp.bfloat16)))
        back = sum_features(
            lax.dot_general(cot, w_down, CONTRACT_COLS, preferred_element_type=jnp.float32)
            * (1.0 / math.sqrt(D))
        )
        dgate = back * up_sum * sigmoid_gate * (1.0 + gate_sum * (1.0 - sigmoid_gate))
        grads = jnp.concatenate([dgate, back * active], axis=1).astype(jnp.bfloat16)
        grads_all.append(gather_units(grads))

    def ascend(weight, left, right):
        grad = (
            lax.dot_general(left, right, CONTRACT_ROWS, preferred_element_type=jnp.float32)
            * token_scale
        )
        return (weight.astype(jnp.float32) + STEP_SIZE * grad).astype(jnp.bfloat16)

    forget_all = jnp.concatenate(forget, axis=0)
    cotan_all = jnp.concatenate(cotan, axis=0)
    grads = jnp.concatenate(grads_all, axis=0)
    new_gate = ascend(w_gate, forget_all, grads[:, :units])
    new_up = ascend(w_up, forget_all, grads[:, units:])
    new_down = ascend(w_down, jnp.concatenate(hidden_all, axis=0), cotan_all)

    half = retain[0].shape[0] // 2
    hidden_keep = []
    for part in (slice(half, None), slice(0, half)):
        rows = jnp.concatenate([block[part] for block in retain], axis=0)
        gate_keep, up_keep = gate_and_up(rows, new_gate, new_up)
        keep = (gate_keep * jax.nn.sigmoid(gate_keep) * up_keep).astype(jnp.bfloat16)
        hidden_keep.append(gather_units(keep))
    far, near = hidden_keep

    out_scale = 1.0 / math.sqrt(FF)
    columns = new_down.shape[1]
    step = columns // 2
    pieces = []
    for start in range(0, columns, step):
        weight = new_down[:, start : start + step]
        sent = (jnp.dot(far, weight, preferred_element_type=jnp.float32) * out_scale).astype(
            jnp.bfloat16
        )
        moved = [
            swap(sent[k * half : (k + 1) * half], "dp", order[-1])
            for k, order in enumerate(orders)
        ]
        total = jnp.dot(near, weight, preferred_element_type=jnp.float32) * out_scale
        piece = []
        for k, order in enumerate(orders):
            mine = total[k * half : (k + 1) * half] + moved[k].astype(jnp.float32)
            for bit in reversed(order[:-1]):
                middle = mine.shape[0] // 2
                other = swap(mine[middle:].astype(jnp.bfloat16), "dp", bit)
                mine = mine[:middle] + other.astype(jnp.float32)
            piece.append(mine)
        pieces.append(jnp.concatenate(piece, axis=0))
    retained = jnp.concatenate(pieces, axis=1).astype(jnp.bfloat16)
    return (retained, new_gate, new_up, new_down)


def solution(mesh):
    in_specs = (
        P("dp", "mp"),
        P("dp", "mp"),
        P("dp", "mp"),
        P("mp", "dp"),
        P("mp", "dp"),
        P("dp", "mp"),
    )
    out_specs = (P("dp", "mp"), P("mp", "dp"), P("mp", "dp"), P("dp", "mp"))
    return jax.shard_map(body, mesh=mesh, in_specs=in_specs, out_specs=out_specs, check_vma=False)
```

```python
import math

import jax
import jax.numpy as jnp
from jax import lax
from jax.sharding import PartitionSpec as P

D = 8192
FF = 16384


STEP_SIZE = 0.5

CONTRACT_ROWS = (((0,), (0,)), ((), ()))
CONTRACT_COLS = (((1,), (1,)), ((), ()))


def swap(values, axis, bit):
    size = lax.axis_size(axis)
    return lax.ppermute(values, axis, [(i, i ^ bit) for i in range(size)])


def bit_orders(size):
    bits = [1 << k for k in reversed(range(size.bit_length() - 1))]
    return bits, bits[:-2] + bits[:-3:-1]


def exchange_rows(halves, orders, stage):
    return tuple(
        jnp.concatenate([rows, swap(rows, "dp", order[stage])], axis=0)
        for rows, order in zip(halves, orders)
    )


def split_halves(rows):
    half = rows.shape[0] // 2
    return rows[:half], rows[half:]


def sum_features(values):
    if lax.axis_size("mp") != 2:
        return lax.psum_scatter(values, "mp", scatter_dimension=0, tiled=True)
    half = values.shape[0] // 2
    first = lax.axis_index("mp") == 0
    low, high = values[:half], values[half:]
    return jnp.where(first, low, high) + swap(jnp.where(first, high, low), "mp", 1)


def gather_units(values):
    if lax.axis_size("mp") != 2:
        return lax.all_gather(values, "mp", axis=0, tiled=True)
    other = swap(values, "mp", 1)
    first = lax.axis_index("mp") == 0
    return jnp.concatenate([jnp.where(first, values, other), jnp.where(first, other, values)], axis=0)


def project(rows, weight):
    return jnp.dot(rows, weight, preferred_element_type=jnp.float32) * (1.0 / math.sqrt(D))


def body(forget_rows, cotangent, retain_rows, w_gate, w_up, w_down):
    orders = bit_orders(lax.axis_size("dp"))
    total_rows = forget_rows.shape[0] * lax.axis_size("dp")
    token_scale = 1.0 / math.sqrt(total_rows)
    forget, cotan, retain = map(split_halves, (forget_rows, cotangent, retain_rows))
    stages = len(orders[0])
    early = stages - 2
    for stage in range(early):
        forget = exchange_rows(forget, orders, stage)
        forget, cotan, retain = lax.optimization_barrier((forget, cotan, retain))
    for step in range(max(2, early)):
        if step < 2:
            forget = exchange_rows(forget, orders, early + step)
        if step < early:
            cotan = exchange_rows(cotan, orders, step)
        forget, cotan, retain = lax.optimization_barrier((forget, cotan, retain))
    for step in range(max(2, early)):
        if step < 2:
            cotan = exchange_rows(cotan, orders, early + step)
        if step < early:
            retain = exchange_rows(retain, orders, step)
        if step == 1:
            forget, retain = lax.optimization_barrier((forget, retain))
        if step != 1:
            cotan, retain = lax.optimization_barrier((cotan, retain))
    for stage in range(early, stages):
        retain = exchange_rows(retain, orders, stage)

    units = w_gate.shape[1]

    def gate_and_up(rows, gate, up):
        sums = sum_features(jnp.concatenate([project(rows, gate), project(rows, up)], axis=1))
        return sums[:, :units], sums[:, units:]

    hidden_all, grads_all = [], []
    for rows, cot in zip(forget, cotan):
        gate_sum, up_sum = gate_and_up(rows, w_gate, w_up)
        sigmoid_gate = jax.nn.sigmoid(gate_sum)
        active = gate_sum * sigmoid_gate
        hidden_all.append(gather_units((active * up_sum).astype(jnp.bfloat16)))
        back = sum_features(
            lax.dot_general(cot, w_down, CONTRACT_COLS, preferred_element_type=jnp.float32)
            * (1.0 / math.sqrt(D))
        )
        dgate = back * up_sum * sigmoid_gate * (1.0 + gate_sum * (1.0 - sigmoid_gate))
        grads = jnp.concatenate([dgate, back * active], axis=1).astype(jnp.bfloat16)
        grads_all.append(gather_units(grads))

    def ascend(weight, left, right):
        grad = (
            lax.dot_general(left, right, CONTRACT_ROWS, preferred_element_type=jnp.float32)
            * token_scale
        )
        return (weight.astype(jnp.float32) + STEP_SIZE * grad).astype(jnp.bfloat16)

    forget_all = jnp.concatenate(forget, axis=0)
    cotan_all = jnp.concatenate(cotan, axis=0)
    grads = jnp.concatenate(grads_all, axis=0)
    new_gate = ascend(w_gate, forget_all, grads[:, :units])
    new_up = ascend(w_up, forget_all, grads[:, units:])
    new_down = ascend(w_down, jnp.concatenate(hidden_all, axis=0), cotan_all)

    half = retain[0].shape[0] // 2
    hidden_keep = []
    for part in (slice(half, None), slice(0, half)):
        rows = jnp.concatenate([block[part] for block in retain], axis=0)
        gate_keep, up_keep = gate_and_up(rows, new_gate, new_up)
        keep = (gate_keep * jax.nn.sigmoid(gate_keep) * up_keep).astype(jnp.bfloat16)
        hidden_keep.append(gather_units(keep))
    far, near = hidden_keep

    out_scale = 1.0 / math.sqrt(FF)
    columns = new_down.shape[1]
    step = columns // 2
    pieces = []
    for start in range(0, columns, step):
        weight = new_down[:, start : start + step]
        sent = (jnp.dot(far, weight, preferred_element_type=jnp.float32) * out_scale).astype(
            jnp.bfloat16
        )
        moved = [
            swap(sent[k * half : (k + 1) * half], "dp", order[-1])
            for k, order in enumerate(orders)
        ]
        total = jnp.dot(near, weight, preferred_element_type=jnp.float32) * out_scale
        piece = []
        for k, order in enumerate(orders):
            mine = total[k * half : (k + 1) * half] + moved[k].astype(jnp.float32)
            for bit in reversed(order[:-1]):
                middle = mine.shape[0] // 2
                other = swap(mine[middle:].astype(jnp.bfloat16), "dp", bit)
                mine = mine[:middle] + other.astype(jnp.float32)
            piece.append(mine)
        pieces.append(jnp.concatenate(piece, axis=0))
    retained = jnp.concatenate(pieces, axis=1).astype(jnp.bfloat16)
    return (retained, new_gate, new_up, new_down)


def solution(mesh):
    in_specs = (
        P("dp", "mp"),
        P("dp", "mp"),
        P("dp", "mp"),
        P("mp", "dp"),
        P("mp", "dp"),
        P("dp", "mp"),
    )
    out_specs = (P("dp", "mp"), P("mp", "dp"), P("mp", "dp"), P("dp", "mp"))
    return jax.shard_map(body, mesh=mesh, in_specs=in_specs, out_specs=out_specs, check_vma=False)
```

```python
import math

import jax
import jax.numpy as jnp
from jax import lax
from jax.sharding import PartitionSpec as P

D = 8192
FF = 16384


STEP_SIZE = 0.5

CONTRACT_ROWS = (((0,), (0,)), ((), ()))
CONTRACT_COLS = (((1,), (1,)), ((), ()))


def swap(values, axis, bit):
    size = lax.axis_size(axis)
    return lax.ppermute(values, axis, [(i, i ^ bit) for i in range(size)])


def bit_orders(size):
    bits = [1 << k for k in reversed(range(size.bit_length() - 1))]
    return bits, bits[:-2] + bits[:-3:-1]


def exchange_rows(halves, orders, stage):
    return tuple(
        jnp.concatenate([rows, swap(rows, "dp", order[stage])], axis=0)
        for rows, order in zip(halves, orders)
    )


def split_halves(rows):
    half = rows.shape[0] // 2
    return rows[:half], rows[half:]


def sum_features(values):
    if lax.axis_size("mp") != 2:
        return lax.psum_scatter(values, "mp", scatter_dimension=0, tiled=True)
    half = values.shape[0] // 2
    first = lax.axis_index("mp") == 0
    low, high = values[:half], values[half:]
    return jnp.where(first, low, high) + swap(jnp.where(first, high, low), "mp", 1)


def gather_units(values):
    if lax.axis_size("mp") != 2:
        return lax.all_gather(values, "mp", axis=0, tiled=True)
    other = swap(values, "mp", 1)
    first = lax.axis_index("mp") == 0
    return jnp.concatenate([jnp.where(first, values, other), jnp.where(first, other, values)], axis=0)


def project(rows, weight):
    return jnp.dot(rows, weight, preferred_element_type=jnp.float32) * (1.0 / math.sqrt(D))


def body(forget_rows, cotangent, retain_rows, w_gate, w_up, w_down):
    orders = bit_orders(lax.axis_size("dp"))
    total_rows = forget_rows.shape[0] * lax.axis_size("dp")
    token_scale = 1.0 / math.sqrt(total_rows)
    forget, cotan, retain = map(split_halves, (forget_rows, cotangent, retain_rows))
    stages = len(orders[0])
    early = stages - 2
    for stage in range(early):
        forget = exchange_rows(forget, orders, stage)
        forget, cotan, retain = lax.optimization_barrier((forget, cotan, retain))
    for step in range(max(2, early)):
        if step < 2:
            forget = exchange_rows(forget, orders, early + step)
        if step < early:
            cotan = exchange_rows(cotan, orders, step)
        forget, cotan, retain = lax.optimization_barrier((forget, cotan, retain))
    for step in range(max(2, early)):
        if step < 2:
            cotan = exchange_rows(cotan, orders, early + step)
        if step < early:
            retain = exchange_rows(retain, orders, step)
        if step == 1:
            forget, retain = lax.optimization_barrier((forget, retain))
        if step != 1:
            cotan, retain = lax.optimization_barrier((cotan, retain))
    for stage in range(early, stages):
        retain = exchange_rows(retain, orders, stage)

    units = w_gate.shape[1]

    def gate_and_up(rows, gate, up):
        sums = sum_features(jnp.concatenate([project(rows, gate), project(rows, up)], axis=1))
        return sums[:, :units], sums[:, units:]

    hidden_all, grads_all = [], []
    for rows, cot in zip(forget, cotan):
        gate_sum, up_sum = gate_and_up(rows, w_gate, w_up)
        sigmoid_gate = jax.nn.sigmoid(gate_sum)
        active = gate_sum * sigmoid_gate
        hidden_all.append(gather_units((active * up_sum).astype(jnp.bfloat16)))
        back = sum_features(
            lax.dot_general(cot, w_down, CONTRACT_COLS, preferred_element_type=jnp.float32)
            * (1.0 / math.sqrt(D))
        )
        dgate = back * up_sum * sigmoid_gate * (1.0 + gate_sum * (1.0 - sigmoid_gate))
        grads = jnp.concatenate([dgate, back * active], axis=1).astype(jnp.bfloat16)
        grads_all.append(gather_units(grads))

    def ascend(weight, left, right):
        grad = (
            lax.dot_general(left, right, CONTRACT_ROWS, preferred_element_type=jnp.float32)
            * token_scale
        )
        return (weight.astype(jnp.float32) + STEP_SIZE * grad).astype(jnp.bfloat16)

    forget_all = jnp.concatenate(forget, axis=0)
    cotan_all = jnp.concatenate(cotan, axis=0)
    new_down = ascend(w_down, jnp.concatenate(hidden_all, axis=0), cotan_all)
    grads, new_down = lax.optimization_barrier((jnp.concatenate(grads_all, axis=0), new_down))
    new_gate = ascend(w_gate, forget_all, grads[:, :units])
    new_up = ascend(w_up, forget_all, grads[:, units:])

    half = retain[0].shape[0] // 2
    hidden_keep = []
    for part in (slice(half, None), slice(0, half)):
        rows = jnp.concatenate([block[part] for block in retain], axis=0)
        gate_keep, up_keep = gate_and_up(rows, new_gate, new_up)
        keep = (gate_keep * jax.nn.sigmoid(gate_keep) * up_keep).astype(jnp.bfloat16)
        hidden_keep.append(gather_units(keep))
    far, near = hidden_keep

    out_scale = 1.0 / math.sqrt(FF)
    columns = new_down.shape[1]
    step = columns // 2
    pieces = []
    ahead = None

    def finish(halves):
        piece = []
        for mine, order in zip(halves, orders):
            for bit in reversed(order[:-1]):
                middle = mine.shape[0] // 2
                other = swap(mine[middle:].astype(jnp.bfloat16), "dp", bit)
                mine = mine[:middle] + other.astype(jnp.float32)
            piece.append(mine)
        return jnp.concatenate(piece, axis=0)

    for start in range(0, columns, step):
        weight = new_down[:, start : start + step]
        sent = (jnp.dot(far, weight, preferred_element_type=jnp.float32) * out_scale).astype(
            jnp.bfloat16
        )
        if ahead is not None:
            sent, *ahead = lax.optimization_barrier((sent, *ahead))
            pieces.append(finish(ahead))
        moved = [
            swap(sent[k * half : (k + 1) * half], "dp", order[-1])
            for k, order in enumerate(orders)
        ]
        total = jnp.dot(near, weight, preferred_element_type=jnp.float32) * out_scale
        ahead = [
            total[k * half : (k + 1) * half] + moved[k].astype(jnp.float32) for k in range(2)
        ]
    pieces.append(finish(ahead))
    retained = jnp.concatenate(pieces, axis=1).astype(jnp.bfloat16)
    return (retained, new_gate, new_up, new_down)


def solution(mesh):
    in_specs = (
        P("dp", "mp"),
        P("dp", "mp"),
        P("dp", "mp"),
        P("mp", "dp"),
        P("mp", "dp"),
        P("dp", "mp"),
    )
    out_specs = (P("dp", "mp"), P("mp", "dp"), P("mp", "dp"), P("dp", "mp"))
    return jax.shard_map(body, mesh=mesh, in_specs=in_specs, out_specs=out_specs, check_vma=False)
```
